32 devices in a mesh: group: 2 (over y), pool: 8 (over z, x), tp: 2 (over core).
Axes of the slice: x: 2, y: 2, z: 4, core: 2. Of those that a mesh axis runs over, the one named last changes fastest.
Arguments:
- queries: bfloat16 [64, 16384], P(('group', 'pool'), 'tp'), parts along dimension 0, may hold values from -16 to 16
- keys: bfloat16 [64, 1024, 256], P(('group', 'pool')), parts along dimension 0, may hold values from -6 to 6
- values: bfloat16 [64, 1024, 256], P(('group', 'pool')), parts along dimension 0, may hold values from -6 to 6
- lengths: int32 [64], P(('group', 'pool')), parts along dimension 0, may hold values from 128 to 1024, as said below
- moe_input: bfloat16 [256, 7168], P(('group', 'pool')), parts along dimension 0, may hold values from -6 to 6
- routes: int32 [256, 3], P(('group', 'pool')), parts along dimension 0, may hold values from 0 to 7, all different within a row; in each aligned block of 16 rows (0 to 15, 16 to 31, ...) at most 8 rows name the same one
- gate_level: int32 [256, 3], P(('group', 'pool')), parts along dimension 0, may hold values from 64 to 1024
- w_gate: bfloat16 [8, 7168, 2560], P('pool', None, 'tp'), may hold values from -0.0625 to 0.0625
- w_up: bfloat16 [8, 7168, 2560], P('pool', None, 'tp'), may hold values from -0.0625 to 0.0625
- w_down: bfloat16 [8, 2560, 7168], P('pool', 'tp'), may hold values from -0.125 to 0.125
Outputs:
- context: bfloat16 [64, 16384], P(('group', 'pool'), 'tp'), parts along dimension 0
- moe_output: bfloat16 [256, 7168], P(('group', 'pool'), 'tp'), parts along dimension 0
The draws below stay inside these ranges and needn't reach their ends.
There are 2 independent parts, one for each index of `group`. The reference program is written for one: setup_inputs(seed, part) draws one part's arguments, and reference() takes and returns one part's arrays. A program takes and returns all parts, laid end to end along the dimension named above; an argument that names none is the same for every part. Nothing has to cross between parts.
Inputs may be any that keep to these rules, and one draw needn't show every extreme that they name: `lengths`: some request has all 1024 slots live in every draw. `routes`: the rows of one index of pool name no expert more than 8 times; some expert exactly 8 times.
All inputs are finite; a program needn't handle non-finite values.
Results may differ from the reference program's by a relative error of at most 0.005.
Values may be sent and summed in bfloat16 or wider, within the bound.
No kernel may reach another device: no remote copies, remote signals or barrier semaphores. Data moves between devices by JAX's collectives and lax.ppermute only.
A program may use at most 128 MiB of HBM per device.

```python
import math
import jax
import jax.numpy as jnp
import numpy as np
from jax import lax

D = 7168
HEADS = 64
HDIM = 256
EXP_HID = 2560
EXPERTS = 8
TOP = 3
CTX = 1024
MOE_DEV = 16
CAP = 8
SPAN = 1
REQUESTS = 32
MOE_ROWS = 128
N_POOL = 8


def draw_queries(key, part):
    key = jax.random.fold_in(key, 1)
    result = jnp.clip(jax.random.normal(key, (REQUESTS, HEADS, HDIM), dtype=jnp.float32), -6.0, 6.0)
    return result.reshape(REQUESTS, HEADS * HDIM).astype(jnp.bfloat16)


def draw_keys(key, part):
    key = jax.random.fold_in(key, 2)
    result = jnp.clip(jax.random.normal(key, (REQUESTS, CTX, HDIM), dtype=jnp.float32), -6.0, 6.0)
    return result.astype(jnp.bfloat16)


def draw_lengths(key, part):
    key = jax.random.fold_in(key, 5)
    drawn = jax.random.randint(jax.random.fold_in(key, 1), (REQUESTS,), CTX // 8, CTX + 1)
    full_at = jax.random.randint(jax.random.fold_in(key, 2), (), 0, REQUESTS)
    return jnp.where(jnp.arange(REQUESTS, dtype=jnp.int32) == full_at, CTX, drawn).astype(jnp.int32)


def place_ends(values, stream_key, smallest, high):
    longest = values.shape.index(max(values.shape))
    spots = []
    for shift in (0, 1):
        where = [jax.random.randint(jax.random.fold_in(stream_key, axis), (), 0, length) for axis, length in enumerate(values.shape)]
        where[longest] = (where[longest] + shift) % values.shape[longest]
        spots.append(tuple(where))
    return values.at[spots[0]].set(smallest).at[spots[1]].set(high)


def level_of(stream_key, dims, pieces, least, top_value):
    loudness = 1.0
    for axis_at, parts in pieces:
        heights = jax.random.uniform(jax.random.fold_in(jax.random.fold_in(stream_key, 6), axis_at), (parts,), jnp.float32, least / len(pieces), top_value / len(pieces))
        loudness = loudness * jnp.repeat(jnp.exp(heights), dims[axis_at] // parts).reshape((-1,) + (1,) * (len(dims) - 1 - axis_at))
    return loudness


def shared_out(key, own, number, rows, amount, top, bound, skew):
    order = jax.random.permutation(key, amount)
    crowded, usual = shares(amount, rows * top, bound, skew, True), shares(amount, rows * top, bound, skew, False)
    places = jnp.arange(amount)

    def named(sizes, rotation):
        used = int((sizes > 0).sum())
        fixed = max(1, used // 4)
        shifted = fixed + (places - fixed + rotation * (used - fixed)) % max(1, amount - fixed)
        return jnp.zeros((amount,), jnp.int32).at[order[jnp.where(places < fixed, places, shifted)]].set(jnp.asarray(sizes, jnp.int32))

    sizes = jnp.where(number % 4 == 0, named(crowded, number // 4), named(usual, number - number // 4 - 1))
    mixed = jax.random.permutation(jax.random.fold_in(own, 3), amount)
    source_of, taker = mixed[0:amount // 2 * 2:2], mixed[1:amount // 2 * 2:2]
    slack = jnp.minimum(sizes[source_of] - 1, bound - sizes[taker]) // 2
    slack = jnp.where((source_of == order[0]) | (taker == order[0]) | (sizes[taker] == 0), 0, jnp.maximum(slack, 0))
    shifted = jax.random.randint(jax.random.fold_in(own, 4), (amount // 2,), 0, 1 << 20) % (slack + 1)
    sizes = sizes.at[source_of].add(-shifted).at[taker].add(shifted)
    members = jnp.searchsorted(jnp.cumsum(sizes), jnp.arange(rows * top), side="right").astype(jnp.int32)
    listing = members.reshape(top, rows).T
    listing = listing[jax.random.permutation(jax.random.fold_in(own, 1), rows)]
    rotation = jax.random.randint(jax.random.fold_in(own, 2), (rows, 1), 0, top)
    return jnp.take_along_axis(listing, (jnp.arange(top)[None, :] + rotation) % top, axis=1)


def shares(count, total, most, lean, full):
    portions = [(1 << 20) // math.isqrt(rank ** lean) + 1 for rank in range(1, count + 1)]
    largest = most if full else min(most, max(-(-total // count), total * portions[0] // sum(portions)))
    least = 1 if total - largest >= count - 1 else 0
    counts, spare = [largest] + [least] * (count - 1), total - largest - least * (count - 1)
    while spare > 0:
        candidates = [i for i in range(1, count) if counts[i] < largest] or [i for i in range(1, count) if counts[i] < most]
        pool, remaining = sum([portions[i] for i in candidates]), spare
        for i in candidates:
            addition = min(most - counts[i], max(1, remaining * portions[i] // pool), spare)
            counts[i] = counts[i] + addition
            spare = spare - addition
    return np.array(counts)


def scatter_about(own_key, shape, width, limit, shards=(), held_as=jnp.bfloat16):
    array = jax.random.normal(own_key, shape, jnp.float32) * width
    if len(shards) > 0:
        array = level_of(own_key, shape, shards, -0.22, 0.18) * array
    return jnp.clip(array, min=-limit, max=limit).astype(held_as)


def setup_inputs(seed: int = 0, part: int = 0) -> dict:
    streams_of = jax.random.split(jax.random.key(seed), 11)
    part_keys = jax.random.split(jax.random.fold_in(streams_of[10], part), 11)
    queries = draw_queries(jax.random.fold_in(jax.random.fold_in(streams_of[10], part), 71), part)
    keys = draw_keys(jax.random.fold_in(jax.random.fold_in(streams_of[10], part), 71), part)
    values = scatter_about(part_keys[2], (REQUESTS, CTX, HDIM), 1.0, 6.0, ((0, 8),))
    lengths = draw_lengths(jax.random.fold_in(jax.random.fold_in(streams_of[10], part), 71), part)
    moe_input = scatter_about(part_keys[4], (MOE_ROWS, D), 1.0, 6.0, ((0, 8),))
    routes_keys = jax.random.split(jax.random.fold_in(part_keys[5], 1), MOE_ROWS // MOE_DEV)
    routes_turns = jax.random.permutation(jax.random.fold_in(part_keys[5], 3), MOE_ROWS // MOE_DEV)
    routes = jax.vmap(lambda own, number: shared_out(jax.random.fold_in(part_keys[5], 2), own, number, MOE_DEV, EXPERTS, TOP, CAP, 2))(routes_keys, routes_turns).reshape((MOE_ROWS, TOP))
    gate_level = place_ends(jax.random.randint(part_keys[6], (MOE_ROWS, TOP), 64, 1025), jax.random.fold_in(part_keys[6], 1), 64, 1024).astype(jnp.int32)
    w_gate = scatter_about(streams_of[7], (N_POOL, D, EXP_HID // SPAN), D ** -0.5, 0.0625, ((0, 8), (2, 2)))
    w_up = scatter_about(streams_of[8], (N_POOL, D, EXP_HID // SPAN), D ** -0.5, 0.0625, ((0, 8), (2, 2)))
    w_down = scatter_about(streams_of[9], (N_POOL, EXP_HID // SPAN, D), EXP_HID ** -0.5, 0.125, ((0, 8), (1, 2)))
    return dict(queries=queries, keys=keys, values=values, lengths=lengths, moe_input=moe_input, routes=routes, gate_level=gate_level, w_gate=w_gate, w_up=w_up, w_down=w_down)


def reference(queries, keys, values, lengths, moe_input, routes, gate_level, w_gate, w_up, w_down):
    scale = HDIM ** -0.5
    query_heads = queries.reshape(REQUESTS, HEADS, HDIM)

    def attend(item):
        query_rows, key_rows, value_rows, length = item
        scores = jnp.dot(query_rows, key_rows.T, preferred_element_type=jnp.float32) * scale
        live = jnp.arange(CTX, dtype=jnp.int32) < length
        scores = jnp.where(live[None, :], scores, -1e30)
        top = jnp.max(scores, axis=1, keepdims=True)
        weights = jnp.exp(scores - top)
        total = jnp.sum(weights, axis=1, keepdims=True)
        summed = jnp.dot(weights.astype(jnp.bfloat16), value_rows, preferred_element_type=jnp.float32)
        return (summed / total).astype(jnp.bfloat16).reshape(HEADS * HDIM)

    context = lax.map(attend, (query_heads, keys, values, lengths))

    capacity = MOE_DEV // 2
    slab = EXP_HID // SPAN
    block_routes = routes.reshape(N_POOL, MOE_DEV * TOP)
    onehot = (block_routes[:, :, None] == jnp.arange(EXPERTS, dtype=jnp.int32)[None, None, :]).astype(jnp.int32)
    earlier = jnp.cumsum(onehot, axis=1) - onehot
    rank = jnp.sum(onehot * earlier, axis=2)
    block_index = jnp.arange(N_POOL, dtype=jnp.int32)[:, None]
    slot = (block_routes * (N_POOL * capacity) + block_index * capacity + rank).reshape(-1).astype(jnp.int32)
    row_of = (jnp.arange(MOE_ROWS * TOP, dtype=jnp.int32) // TOP).astype(jnp.int32)
    table = jnp.full((EXPERTS * N_POOL * capacity,), MOE_ROWS, dtype=jnp.int32).at[slot].set(row_of)
    padded = jnp.concatenate([moe_input, jnp.zeros((1, D), moe_input.dtype)], axis=0)
    expert_input = padded[table].reshape(EXPERTS, N_POOL * capacity, D)

    gate_full = w_gate.reshape(EXPERTS, SPAN, D, slab).transpose(0, 2, 1, 3).reshape(EXPERTS, D, EXP_HID)
    up_full = w_up.reshape(EXPERTS, SPAN, D, slab).transpose(0, 2, 1, 3).reshape(EXPERTS, D, EXP_HID)
    down_full = w_down.reshape(EXPERTS, EXP_HID, D)

    def expert(item):
        rows, gate_mat, up_mat, down_mat = item
        gate = jnp.dot(rows, gate_mat, preferred_element_type=jnp.float32)
        upper = jnp.dot(rows, up_mat, preferred_element_type=jnp.float32)
        hidden = (jax.nn.silu(gate) * upper).astype(jnp.bfloat16)
        return jnp.dot(hidden, down_mat, preferred_element_type=jnp.float32)

    expert_output = lax.map(expert, (expert_input, gate_full, up_full, down_full)).reshape(-1, D)
    picked = expert_output[slot].reshape(MOE_ROWS, TOP, D)
    gate_weight = gate_level.astype(jnp.float32) / 1024.0
    moe_output = jnp.sum(picked * gate_weight[:, :, None], axis=1).astype(jnp.bfloat16)
    return context, moe_output
```

```python
import functools

import jax
import jax.numpy as jnp
from jax import lax
from jax.experimental import pallas as pl
from jax.experimental.pallas import tpu as pltpu
from jax.sharding import PartitionSpec as P

HDIM = 256
EXPERTS = 8
TOP = 3
MIB = 2**20
SWAP = [(0, 1), (1, 0)]
VMEM = pltpu.VMEM
BF16 = jnp.bfloat16
F32 = jnp.float32


def distances(count):
    pairs, top = [], count // 2
    while top >= 2:
        half = top // 2
        pairs += [(top + i, top + half + i) for i in range(half)]
        top //= 2
    return pairs


def route_of(count, pair):
    return [
        (p * 2 + c, (p ^ pair[c]) * 2 + c) for p in range(count) for c in range(2)
    ]


def attention(queries, keys, values, lengths):
    requests_here = queries.shape[0]
    heads_here = queries.shape[1] // HDIM
    query_heads = queries.reshape(requests_here, heads_here, HDIM)
    scores = jnp.einsum(
        "rhd,rkd->rhk", query_heads, keys, preferred_element_type=jnp.float32
    ) * HDIM ** (-0.5)
    live = jnp.arange(keys.shape[1], dtype=jnp.int32)[None, :] < lengths[:, None]
    scores = jnp.where(live[:, None, :], scores, -1e30)
    top = jnp.max(scores, axis=2, keepdims=True)
    weights = jnp.exp(scores - top)
    total = jnp.sum(weights, axis=2, keepdims=True)
    summed = jnp.einsum(
        "rhk,rkd->rhd", weights.astype(jnp.bfloat16), values, preferred_element_type=jnp.float32
    )
    return (summed / total).astype(jnp.bfloat16).reshape(requests_here, heads_here * HDIM)


def places(routes, levels, ks, span, capacity):
    rows = routes.shape[1]
    me = lax.axis_index("pool")
    slots = len(ks) * capacity
    slot = lax.broadcasted_iota(jnp.int32, (slots, 1), 0)
    expert = jnp.zeros((slots, 1), jnp.int32)
    for i, k in enumerate(ks):
        named = lax.bitwise_xor(me, k)
        if span > 1:
            named = lax.div(named, span)
        expert = jnp.where(slot >= i * capacity, named, expert)
    chosen = jnp.zeros((slots, rows), jnp.bool_)
    level = jnp.zeros((slots, rows), jnp.int32)
    for t in range(TOP):
        same = routes[t : t + 1, :] == expert
        chosen = jnp.logical_or(chosen, same)
        if levels is not None:
            level = level + jnp.where(same, levels[t : t + 1, :], 0)
    before = lax.broadcasted_iota(jnp.int32, (rows, rows), 0) < lax.broadcasted_iota(
        jnp.int32, (rows, rows), 1
    )
    rank = jnp.dot(
        jnp.where(chosen, 1.0, 0.0).astype(BF16),
        jnp.where(before, 1.0, 0.0).astype(BF16),
        preferred_element_type=F32,
    )
    place = lax.rem(slot, capacity).astype(F32)
    here = jnp.logical_and(chosen, rank == place)
    return here, level


def dispatch_kernel(pairs, span, capacity, routes_ref, x_ref, *outs):
    core = lax.axis_index("tp")
    half = x_ref.shape[1] // 2
    ks = [jnp.where(core == 0, a, b) for a, b in pairs] + [1, 0]
    here, _ = places(routes_ref[...], None, ks, span, capacity)
    picks = jnp.where(here, 1.0, 0.0).astype(BF16)
    m = len(pairs)
    full = jnp.dot(picks, x_ref[...], preferred_element_type=F32)
    for i in range(m):
        outs[i][...] = full[i * capacity : (i + 1) * capacity].astype(BF16)
    outs[m + 1][...] = full[(m + 1) * capacity :].astype(BF16)
    mine = x_ref[:, pl.ds(pl.multiple_of(core * half, 128), half)]
    outs[m][...] = jnp.dot(
        picks[m * capacity : (m + 1) * capacity], mine, preferred_element_type=F32
    ).astype(BF16)


def expert_kernel(m, capacity, *refs):
    blocks = refs[: 2 * m]
    share_mine, share_theirs, own, gate_hbm, up_hbm, down_hbm, keep, give = refs[2 * m : 2 * m + 8]
    x, gate_w, up_w, down_w, total, result, hidden, gate_sem, up_sem, down_sem = refs[2 * m + 8 :]
    core = lax.axis_index("tp")
    depth, width = gate_w.shape
    half = depth // 2
    steps, parts = gate_sem.shape[0], down_sem.shape[0]
    deep, wide = depth // steps, width // parts

    def fetch(source, target, sem, size, i):
        at = pl.ds(i * size, size)
        return pltpu.make_async_copy(source.at[at], target.at[at], sem.at[i])

    for i in range(steps):
        fetch(gate_hbm, gate_w, gate_sem, deep, i).start()
        fetch(up_hbm, up_w, up_sem, deep, i).start()
    for i in range(parts):
        fetch(down_hbm, down_w, down_sem, wide, i).start()
    two = 2 * capacity
    for i in range(m):
        x[i * two : (i + 1) * two, :] = jnp.concatenate(
            [blocks[2 * i][...], blocks[2 * i + 1][...]], axis=0
        )
    for c, part in ((core, share_mine), (1 - core, share_theirs)):
        at = pl.ds(pl.multiple_of(c * half, 128), half)
        x[m * two : (m + 1) * two, at] = jnp.concatenate([part[...], own[:, at]], axis=0)
    for i in range(steps):
        rows = x[:, i * deep : (i + 1) * deep]
        for j, (weight, source, sem) in enumerate(
            ((gate_w, gate_hbm, gate_sem), (up_w, up_hbm, up_sem))
        ):
            fetch(source, weight, sem, deep, i).wait()
            term = jnp.dot(
                rows, weight[i * deep : (i + 1) * deep, :], preferred_element_type=F32
            )
            total[j] = term if i == 0 else total[j] + term
    gate = total[0]
    hidden[...] = (gate / (1.0 + jnp.exp(-gate)) * total[1]).astype(BF16)
    for i in range(parts):
        fetch(down_hbm, down_w, down_sem, wide, i).wait()
        term = jnp.dot(
            hidden[:, i * wide : (i + 1) * wide],
            down_w[i * wide : (i + 1) * wide, :],
            preferred_element_type=F32,
        )
        result[...] = term if i == 0 else result[...] + term
    n = m * capacity
    keep[:n, :] = result[:n, :]
    mine = pl.ds(pl.multiple_of(core * half, 128), half)
    theirs = pl.ds(pl.multiple_of((1 - core) * half, 128), half)
    keep[n:, :half] = result[2 * n : 2 * n + capacity, mine]
    keep[n:, half:] = result[2 * n + capacity :, mine]
    rest = jnp.concatenate(
        [result[2 * n : 2 * n + capacity, theirs], result[2 * n + capacity :, theirs]], axis=1
    )
    give[...] = jnp.concatenate([result[n : 2 * n, :], rest], axis=0).astype(BF16)


def sum_kernel(m, capacity, keep, got, *outs):
    both = keep[...] + got[...].astype(F32)
    half = keep.shape[1] // 2
    for i in range(m):
        outs[i][...] = both[i * capacity : (i + 1) * capacity].astype(BF16)
    outs[m][...] = both[m * capacity :, :half].astype(BF16)
    outs[m + 1][...] = both[m * capacity :, half:].astype(BF16)


def combine_kernel(pairs, span, capacity, routes_ref, level_ref, *refs):
    m = len(pairs)
    blocks, shared, own, out = refs[: 2 * m], refs[2 * m], refs[2 * m + 1], refs[2 * m + 2]
    core = lax.axis_index("tp")
    half = out.shape[1]
    ks = [jnp.where(core == 0, a, b) for a, b in pairs]
    ks += [jnp.where(core == 0, b, a) for a, b in pairs] + [1, 0]
    here, level = places(routes_ref[...], level_ref[...], ks, span, capacity)
    weight = jnp.where(here, level, 0).astype(F32) / 1024.0
    high = weight.astype(BF16)
    low = (weight - high.astype(F32)).astype(BF16)
    at = pl.ds(pl.multiple_of(core * half, 128), half)
    held = jnp.concatenate([b[:, at] for b in blocks] + [shared[...], own[...]], axis=0)
    dims = (((0,), (0,)), ((), ()))
    out[...] = (
        lax.dot_general(high, held, dims, preferred_element_type=F32)
        + lax.dot_general(low, held, dims, preferred_element_type=F32)
    ).astype(BF16)


def body(queries, keys, values, lengths, moe_input, routes, gate_level, w_gate, w_up, w_down):
    count = lax.axis_size("pool")
    span = count // EXPERTS
    rows_here, width = moe_input.shape
    capacity = rows_here // 2
    half = width // 2
    hid = w_gate.shape[2]
    pairs = distances(count)
    m = len(pairs)
    axes = ("pool", "tp")
    routes_t, level_t = routes.T, gate_level.T

    block = jax.ShapeDtypeStruct((capacity, width), BF16)
    half_block = jax.ShapeDtypeStruct((capacity, half), BF16)
    in_vmem = pl.BlockSpec(memory_space=VMEM)
    *sent, shared, own = pl.pallas_call(
        functools.partial(dispatch_kernel, pairs, span, capacity),
        out_shape=[block] * m + [half_block, block],
        in_specs=[in_vmem] * 2,
        out_specs=[in_vmem] * (m + 2),
        compiler_params=pltpu.CompilerParams(vmem_limit_bytes=(12 if m < 8 else 40) * MIB),
        name="dispatch",
    )(routes_t, moe_input)

    mine = [lax.ppermute(b, axes, route_of(count, pair)) for b, pair in zip(sent, pairs)]
    share_mine = lax.ppermute(shared, axes, route_of(count, (1, 1)))
    theirs = [lax.ppermute(b, "tp", SWAP) for b in mine]
    share_theirs = lax.ppermute(share_mine, "tp", SWAP)

    context = attention(queries, keys, values, lengths)

    total_rows = count * capacity
    steps = 14
    parts = hid // 256 if hid % 256 == 0 else 1
    weight_bytes = 3 * width * hid * 2
    keep, give = pl.pallas_call(
        functools.partial(expert_kernel, m, capacity),
        out_shape=[
            jax.ShapeDtypeStruct(((m + 1) * capacity, width), F32),
            jax.ShapeDtypeStruct(((m + 1) * capacity, width), BF16),
        ],
        in_specs=[in_vmem] * (2 * m + 3) + [pl.BlockSpec(memory_space=pl.ANY)] * 3,
        out_specs=[in_vmem] * 2,
        scratch_shapes=[
            VMEM((total_rows, width), BF16),
            VMEM((width, hid), BF16),
            VMEM((width, hid), BF16),
            VMEM((hid, width), BF16),
            VMEM((2, total_rows, hid), F32),
            VMEM((total_rows, width), F32),
            VMEM((total_rows, hid), BF16),
            pltpu.SemaphoreType.DMA((steps,)),
            pltpu.SemaphoreType.DMA((steps,)),
            pltpu.SemaphoreType.DMA((parts,)),
        ],
        compiler_params=pltpu.CompilerParams(vmem_limit_bytes=60 * MIB),
        cost_estimate=pl.CostEstimate(
            flops=2 * total_rows * 3 * width * hid, bytes_accessed=weight_bytes, transcendentals=0
        ),
        name="experts",
    )(*mine, *theirs, share_mine, share_theirs, own, w_gate[0], w_up[0], w_down[0])

    got = lax.ppermute(give, "tp", SWAP)
    *back, share_back, own_back = pl.pallas_call(
        functools.partial(sum_kernel, m, capacity),
        out_shape=[block] * m + [half_block] * 2,
        in_specs=[in_vmem] * 2,
        out_specs=[in_vmem] * (m + 2),
        compiler_params=pltpu.CompilerParams(vmem_limit_bytes=(12 if m < 8 else 40) * MIB),
        name="sum",
    )(keep, got)

    mine = [lax.ppermute(b, axes, route_of(count, pair)) for b, pair in zip(back, pairs)]
    share_back = lax.ppermute(share_back, axes, route_of(count, (1, 1)))
    theirs = [lax.ppermute(b, "tp", SWAP) for b in mine]
    moe_output = pl.pallas_call(
        functools.partial(combine_kernel, pairs, span, capacity),
        out_shape=jax.ShapeDtypeStruct((rows_here, half), BF16),
        in_specs=[in_vmem] * (2 * m + 4),
        out_specs=in_vmem,
        compiler_params=pltpu.CompilerParams(vmem_limit_bytes=(12 if m < 8 else 40) * MIB),
        name="combine",
    )(routes_t, level_t, *mine, *theirs, share_back, own_back)
    return (context, moe_output)


def solution(mesh):
    return jax.shard_map(
        body,
        mesh=mesh,
        in_specs=(
            P(("group", "pool"), "tp"),
            P(("group", "pool"), None, None),
            P(("group", "pool"), None, None),
            P(("group", "pool")),
            P(("group", "pool"), None),
            P(("group", "pool"), None),
            P(("group", "pool"), None),
            P("pool", None, "tp"),
            P("pool", None, "tp"),
            P("pool", "tp", None),
        ),
        out_specs=(P(("group", "pool"), "tp"), P(("group", "pool"), "tp")),
        check_vma=False,
    )
```

```python
import functools

import jax
import jax.numpy as jnp
from jax import lax
from jax.experimental import pallas as pl
from jax.experimental.pallas import tpu as pltpu
from jax.sharding import PartitionSpec as P

HDIM = 256
EXPERTS = 8
TOP = 3
MIB = 2**20
HEAD = 1024
SWAP = [(0, 1), (1, 0)]
VMEM = pltpu.VMEM
BF16 = jnp.bfloat16
F32 = jnp.float32


def distances(count):
    pairs, top = [], count // 2
    while top >= 2:
        half = top // 2
        pairs += [(top + i, top + half + i) for i in range(half)]
        top //= 2
    return pairs


def route_of(count, pair):
    return [
        (p * 2 + c, (p ^ pair[c]) * 2 + c) for p in range(count) for c in range(2)
    ]


def attention_kernel(loads, *refs):
    n = len(loads)
    sources, weights, out_ref, held = refs[:4], refs[4:6], refs[6], refs[7 : 7 + n]
    lengths_ref, q_ref, k_ref, v_ref, packed, mixed, own_sems, sems = refs[7 + n :]
    own = [
        pltpu.make_async_copy(source, ref, own_sems.at[i])
        for i, (source, ref) in enumerate(zip(sources, (lengths_ref, q_ref, k_ref, v_ref)))
    ]
    for copy in own:
        copy.start()
    copies = []
    for i, (which, start, rows) in enumerate(loads):
        copy = pltpu.make_async_copy(
            weights[which].at[pl.ds(start, rows)], held[i], sems.at[i]
        )
        copy.start()
        copies.append(copy)
    requests, slots, size = k_ref.shape
    heads = q_ref.shape[1] // size
    planes = packed.shape[0]
    own[0].wait()
    own[1].wait()
    for i in range(heads * planes):
        h, j = divmod(i, planes)
        packed[j, h * requests : (h + 1) * requests, :] = q_ref[:, i * 128 : (i + 1) * 128].astype(
            F32
        )
    own[2].wait()
    own[3].wait()
    for r in range(requests):
        every = pl.ds(r, heads, stride=requests)
        query = jnp.concatenate([packed[j, every, :] for j in range(planes)], axis=1).astype(BF16)
        scores = lax.dot_general(
            query, k_ref[r], (((1,), (1,)), ((), ())), preferred_element_type=F32
        ) * size ** (-0.5)
        live = lax.broadcasted_iota(jnp.int32, (1, slots), 1) < lengths_ref[r]
        scores = jnp.where(live, scores, -1e30)
        weight = jnp.exp(scores - jnp.max(scores, axis=1, keepdims=True))
        total = jnp.sum(weight, axis=1, keepdims=True)
        result = jnp.dot(weight.astype(BF16), v_ref[r], preferred_element_type=F32) / total
        for j in range(planes):
            mixed[j, every, :] = result[:, j * 128 : (j + 1) * 128]
    for i in range(heads * planes):
        h, j = divmod(i, planes)
        out_ref[:, i * 128 : (i + 1) * 128] = mixed[
            j, h * requests : (h + 1) * requests, :
        ].astype(BF16)
    for copy in copies:
        copy.wait()


def places(routes, levels, ks, span, capacity):
    rows = routes.shape[1]
    me = lax.axis_index("pool")
    slots = len(ks) * capacity
    slot = lax.broadcasted_iota(jnp.int32, (slots, 1), 0)
    expert = jnp.zeros((slots, 1), jnp.int32)
    for i, k in enumerate(ks):
        named = lax.bitwise_xor(me, k)
        if span > 1:
            named = lax.div(named, span)
        expert = jnp.where(slot >= i * capacity, named, expert)
    chosen = jnp.zeros((slots, rows), jnp.bool_)
    level = jnp.zeros((slots, rows), jnp.int32)
    for t in range(TOP):
        same = routes[t : t + 1, :] == expert
        chosen = jnp.logical_or(chosen, same)
        if levels is not None:
            level = level + jnp.where(same, levels[t : t + 1, :], 0)
    before = lax.broadcasted_iota(jnp.int32, (rows, rows), 0) < lax.broadcasted_iota(
        jnp.int32, (rows, rows), 1
    )
    rank = jnp.dot(
        jnp.where(chosen, 1.0, 0.0).astype(BF16),
        jnp.where(before, 1.0, 0.0).astype(BF16),
        preferred_element_type=F32,
    )
    place = lax.rem(slot, capacity).astype(F32)
    here = jnp.logical_and(chosen, rank == place)
    return here, level


def dispatch_kernel(pairs, span, capacity, routes_hbm, x_hbm, *refs):
    *outs, routes_ref, x_ref, sems = refs
    get_routes = pltpu.make_async_copy(routes_hbm, routes_ref, sems.at[0])
    get_x = pltpu.make_async_copy(x_hbm, x_ref, sems.at[1])
    get_routes.start()
    get_x.start()
    get_routes.wait()
    core = lax.axis_index("tp")
    half = x_ref.shape[1] // 2
    ks = [jnp.where(core == 0, a, b) for a, b in pairs] + [1, 0]
    here, _ = places(routes_ref[...], None, ks, span, capacity)
    picks = jnp.where(here, 1.0, 0.0).astype(BF16)
    m = len(pairs)
    get_x.wait()
    full = jnp.dot(picks, x_ref[...], preferred_element_type=F32)
    for i in range(m):
        outs[i][...] = full[i * capacity : (i + 1) * capacity].astype(BF16)
    outs[m + 1][...] = full[(m + 1) * capacity :].astype(BF16)
    mine = x_ref[:, pl.ds(pl.multiple_of(core * half, 128), half)]
    outs[m][...] = jnp.dot(
        picks[m * capacity : (m + 1) * capacity], mine, preferred_element_type=F32
    ).astype(BF16)


def expert_kernel(m, capacity, plan, *refs):
    blocks = refs[: 2 * m]
    share_mine, share_theirs, own = refs[2 * m : 2 * m + 3]
    held = sum(i >= 0 for ranges in plan for _, _, i in ranges)
    at = 2 * m + 3
    parts_held, refs = refs[at : at + held], refs[at + held :]
    gate_hbm, up_hbm, down_hbm, keep, give = refs[:5]
    x, rest_w, down_w, total, result, hidden, rest_sem, down_sem = refs[5:]
    core = lax.axis_index("tp")
    depth, width = x.shape[1], hidden.shape[1]
    half = depth // 2
    wide, ring = down_w.shape[1], down_w.shape[0]
    parts = width // wide

    fetches, place = {}, 0
    for j, (ranges, source) in enumerate(zip(plan, (gate_hbm, up_hbm))):
        for start, rows, i in ranges:
            if i < 0:
                fetches[j, start] = (
                    place,
                    pltpu.make_async_copy(
                        source.at[pl.ds(start, rows)],
                        rest_w.at[pl.ds(place, rows)],
                        rest_sem.at[len(fetches)],
                    ),
                )
                place += rows
    for _, copy in fetches.values():
        copy.start()

    def fetch(i):
        return pltpu.make_async_copy(
            down_hbm.at[pl.ds(i * wide, wide)], down_w.at[i % ring], down_sem.at[i]
        )

    for i in range(min(ring, parts)):
        fetch(i).start()
    two = 2 * capacity
    for i in range(m):
        x[i * two : (i + 1) * two, :] = jnp.concatenate(
            [blocks[2 * i][...], blocks[2 * i + 1][...]], axis=0
        )
    for c, part in ((core, share_mine), (1 - core, share_theirs)):
        at = pl.ds(pl.multiple_of(c * half, 128), half)
        x[m * two : (m + 1) * two, at] = jnp.concatenate([part[...], own[:, at]], axis=0)
    for j, ranges in enumerate(plan):
        for start, rows, i in ranges:
            if i < 0:
                place, copy = fetches[j, start]
                copy.wait()
                weight = rest_w[place : place + rows, :]
            else:
                weight = parts_held[i][...]
            term = jnp.dot(x[:, start : start + rows], weight, preferred_element_type=F32)
            total[j] = term if start == 0 else total[j] + term
    gate = total[0]
    hidden[...] = (gate / (1.0 + jnp.exp(-gate)) * total[1]).astype(BF16)
    for i in range(parts):
        fetch(i).wait()
        term = jnp.dot(
            hidden[:, i * wide : (i + 1) * wide], down_w[i % ring], preferred_element_type=F32
        )
        result[...] = term if i == 0 else result[...] + term
        if i + ring < parts:
            fetch(i + ring).start()
    n = m * capacity
    keep[:n, :] = result[:n, :]
    mine = pl.ds(pl.multiple_of(core * half, 128), half)
    theirs = pl.ds(pl.multiple_of((1 - core) * half, 128), half)
    keep[n:, :half] = result[2 * n : 2 * n + capacity, mine]
    keep[n:, half:] = result[2 * n + capacity :, mine]
    rest = jnp.concatenate(
        [result[2 * n : 2 * n + capacity, theirs], result[2 * n + capacity :, theirs]], axis=1
    )
    give[...] = jnp.concatenate([result[n : 2 * n, :], rest], axis=0).astype(BF16)


def sum_kernel(m, capacity, keep, got, *outs):
    both = keep[...] + got[...].astype(F32)
    half = keep.shape[1] // 2
    for i in range(m):
        outs[i][...] = both[i * capacity : (i + 1) * capacity].astype(BF16)
    outs[m][...] = both[m * capacity :, :half].astype(BF16)
    outs[m + 1][...] = both[m * capacity :, half:].astype(BF16)


def combine_kernel(pairs, span, capacity, routes_ref, level_ref, *refs):
    m = len(pairs)
    blocks, shared, own, out = refs[: 2 * m], refs[2 * m], refs[2 * m + 1], refs[2 * m + 2]
    core = lax.axis_index("tp")
    half = out.shape[1]
    ks = [jnp.where(core == 0, a, b) for a, b in pairs]
    ks += [jnp.where(core == 0, b, a) for a, b in pairs] + [1, 0]
    here, level = places(routes_ref[...], level_ref[...], ks, span, capacity)
    weight = jnp.where(here, level, 0).astype(F32) / 1024.0
    high = weight.astype(BF16)
    low = (weight - high.astype(F32)).astype(BF16)
    at = pl.ds(pl.multiple_of(core * half, 128), half)
    held = jnp.concatenate([b[:, at] for b in blocks] + [shared[...], own[...]], axis=0)
    dims = (((0,), (0,)), ((), ()))
    out[...] = (
        lax.dot_general(high, held, dims, preferred_element_type=F32)
        + lax.dot_general(low, held, dims, preferred_element_type=F32)
    ).astype(BF16)


def body(queries, keys, values, lengths, moe_input, routes, gate_level, w_gate, w_up, w_down):
    count = lax.axis_size("pool")
    span = count // EXPERTS
    rows_here, width = moe_input.shape
    capacity = rows_here // 2
    half = width // 2
    hid = w_gate.shape[2]
    pairs = distances(count)
    m = len(pairs)
    axes = ("pool", "tp")
    routes_t, level_t = routes.T, gate_level.T
    far = functools.partial(pltpu.with_memory_space_constraint, memory_space=pltpu.HBM)

    block = jax.ShapeDtypeStruct((capacity, width), BF16)
    half_block = jax.ShapeDtypeStruct((capacity, half), BF16)
    in_vmem = pl.BlockSpec(memory_space=VMEM)
    *sent, shared, own = pl.pallas_call(
        functools.partial(dispatch_kernel, pairs, span, capacity),
        out_shape=[block] * m + [half_block, block],
        in_specs=[pl.BlockSpec(memory_space=pltpu.HBM)] * 2,
        out_specs=[in_vmem] * (m + 2),
        scratch_shapes=[
            VMEM(routes_t.shape, jnp.int32),
            VMEM(moe_input.shape, BF16),
            pltpu.SemaphoreType.DMA((2,)),
        ],
        compiler_params=pltpu.CompilerParams(vmem_limit_bytes=(8 if m < 8 else 40) * MIB),
        name="dispatch",
    )(far(routes_t), far(moe_input))

    mine = [lax.ppermute(b, axes, route_of(count, pair)) for b, pair in zip(sent, pairs)]
    share_mine = lax.ppermute(shared, axes, route_of(count, (1, 1)))
    total_rows = count * capacity
    step = width // 14
    roomy = total_rows <= 64
    loads, plan = [], ([], [])
    for j, early in enumerate((width, HEAD) if roomy else (0, 0)):
        for start in range(0, width, step):
            index = -1
            if start < early:
                index = len(loads)
                loads.append((j, start, step))
            plan[j].append((start, step, index))
    gate_hbm, up_hbm, down_hbm = (far(w[0]) for w in (w_gate, w_up, w_down))
    requests, slots, size = keys.shape
    heads = queries.shape[1] // size
    in_hbm = pl.BlockSpec(memory_space=pltpu.HBM)
    early_bytes = 4 * requests * slots * size + 2 * hid * step * len(loads)
    context, *held = pl.pallas_call(
        functools.partial(attention_kernel, loads),
        out_shape=[jax.ShapeDtypeStruct(queries.shape, BF16)]
        + [VMEM((rows, hid), BF16) for _, _, rows in loads],
        in_specs=[in_hbm] * 6,
        out_specs=[in_vmem] * (1 + len(loads)),
        scratch_shapes=[
            pltpu.SMEM(lengths.shape, jnp.int32),
            VMEM(queries.shape, BF16),
            VMEM(keys.shape, BF16),
            VMEM(values.shape, BF16),
            VMEM((size // 128, heads * requests, 128), F32),
            VMEM((size // 128, heads * requests, 128), F32),
            pltpu.SemaphoreType.DMA((4,)),
            pltpu.SemaphoreType.DMA((max(1, len(loads)),)),
        ],
        compiler_params=pltpu.CompilerParams(vmem_limit_bytes=10 * MIB),
        cost_estimate=pl.CostEstimate(
            flops=4 * requests * heads * slots * size,
            bytes_accessed=early_bytes,
            transcendentals=requests * heads * slots,
        ),
        name="attention",
    )(far(lengths), far(queries), far(keys), far(values), gate_hbm, up_hbm)

    *mine, share_mine, context = lax.optimization_barrier((*mine, share_mine, context))
    theirs = [lax.ppermute(b, "tp", SWAP) for b in mine]
    share_theirs = lax.ppermute(share_mine, "tp", SWAP)

    fetched = 2 * 14 - len(loads)
    wide = 256 if hid % 256 == 0 else hid
    parts = hid // wide
    ring = min(parts, 3)
    weight_bytes = 2 * hid * (step * fetched + width)
    keep, give = pl.pallas_call(
        functools.partial(expert_kernel, m, capacity, plan),
        out_shape=[
            jax.ShapeDtypeStruct(((m + 1) * capacity, width), F32),
            jax.ShapeDtypeStruct(((m + 1) * capacity, width), BF16),
        ],
        in_specs=[in_vmem] * (2 * m + 3 + len(held)) + [in_hbm] * 3,
        out_specs=[in_vmem] * 2,
        scratch_shapes=[
            VMEM((total_rows, width), BF16),
            VMEM((step * fetched, hid), BF16),
            VMEM((ring, wide, width), BF16),
            VMEM((2, total_rows, hid), F32),
            VMEM((total_rows, width), F32),
            VMEM((total_rows, hid), BF16),
            pltpu.SemaphoreType.DMA((fetched,)),
            pltpu.SemaphoreType.DMA((parts,)),
        ],
        compiler_params=pltpu.CompilerParams(vmem_limit_bytes=(31 if roomy else 58) * MIB),
        cost_estimate=pl.CostEstimate(
            flops=2 * total_rows * 3 * width * hid, bytes_accessed=weight_bytes, transcendentals=0
        ),
        name="experts",
    )(*mine, *theirs, share_mine, share_theirs, own, *held, gate_hbm, up_hbm, down_hbm)

    got = lax.ppermute(give, "tp", SWAP)
    *back, share_back, own_back = pl.pallas_call(
        functools.partial(sum_kernel, m, capacity),
        out_shape=[block] * m + [half_block] * 2,
        in_specs=[in_vmem] * 2,
        out_specs=[in_vmem] * (m + 2),
        compiler_params=pltpu.CompilerParams(vmem_limit_bytes=(8 if m < 8 else 40) * MIB),
        name="sum",
    )(keep, got)

    mine = [lax.ppermute(b, axes, route_of(count, pair)) for b, pair in zip(back, pairs)]
    share_back = lax.ppermute(share_back, axes, route_of(count, (1, 1)))
    theirs = [lax.ppermute(b, "tp", SWAP) for b in mine]
    moe_output = pl.pallas_call(
        functools.partial(combine_kernel, pairs, span, capacity),
        out_shape=jax.ShapeDtypeStruct((rows_here, half), BF16),
        in_specs=[in_vmem] * (2 * m + 4),
        out_specs=in_vmem,
        compiler_params=pltpu.CompilerParams(vmem_limit_bytes=(8 if m < 8 else 40) * MIB),
        name="combine",
    )(routes_t, level_t, *mine, *theirs, share_back, own_back)
    return (context, moe_output)


def solution(mesh):
    return jax.shard_map(
        body,
        mesh=mesh,
        in_specs=(
            P(("group", "pool"), "tp"),
            P(("group", "pool"), None, None),
            P(("group", "pool"), None, None),
            P(("group", "pool")),
            P(("group", "pool"), None),
            P(("group", "pool"), None),
            P(("group", "pool"), None),
            P("pool", None, "tp"),
            P("pool", None, "tp"),
            P("pool", "tp", None),
        ),
        out_specs=(P(("group", "pool"), "tp"), P(("group", "pool"), "tp")),
        check_vma=False,
    )
```

```python
import functools

import jax
import jax.numpy as jnp
from jax import lax
from jax.experimental import pallas as pl
from jax.experimental.pallas import tpu as pltpu
from jax.sharding import PartitionSpec as P

HDIM = 256
EXPERTS = 8
TOP = 3
MIB = 2**20
HEAD = 1024
AHEAD = 4
SWAP = [(0, 1), (1, 0)]
VMEM = pltpu.VMEM
BF16 = jnp.bfloat16
F32 = jnp.float32


def distances(count):
    pairs, top = [], count // 2
    while top >= 2:
        half = top // 2
        pairs += [(top + i, top + half + i) for i in range(half)]
        top //= 2
    return pairs


def route_of(count, pair):
    return [
        (p * 2 + c, (p ^ pair[c]) * 2 + c) for p in range(count) for c in range(2)
    ]


def attention_kernel(loads, *refs):
    n = len(loads)
    sources, weights, out_ref, held = refs[:4], refs[4:6], refs[6], refs[7 : 7 + n]
    lengths_ref, q_ref, k_ref, v_ref, packed, mixed, own_sems, sems = refs[7 + n :]
    own = [
        pltpu.make_async_copy(source, ref, own_sems.at[i])
        for i, (source, ref) in enumerate(zip(sources, (lengths_ref, q_ref, k_ref, v_ref)))
    ]
    for copy in own:
        copy.start()
    copies = []
    for i, (which, start, rows) in enumerate(loads):
        copy = pltpu.make_async_copy(
            weights[which].at[pl.ds(start, rows)], held[i], sems.at[i]
        )
        copies.append(copy)
    for copy in copies[:AHEAD]:
        copy.start()
    requests, slots, size = k_ref.shape
    heads = q_ref.shape[1] // size
    planes = packed.shape[0]
    own[0].wait()
    own[1].wait()
    for i in range(heads * planes):
        h, j = divmod(i, planes)
        packed[j, h * requests : (h + 1) * requests, :] = q_ref[:, i * 128 : (i + 1) * 128].astype(
            F32
        )
    own[2].wait()
    own[3].wait()
    for copy in copies[AHEAD:]:
        copy.start()
    for r in range(requests):
        every = pl.ds(r, heads, stride=requests)
        query = jnp.concatenate([packed[j, every, :] for j in range(planes)], axis=1).astype(BF16)
        scores = lax.dot_general(
            query, k_ref[r], (((1,), (1,)), ((), ())), preferred_element_type=F32
        ) * size ** (-0.5)
        live = lax.broadcasted_iota(jnp.int32, (1, slots), 1) < lengths_ref[r]
        scores = jnp.where(live, scores, -1e30)
        weight = jnp.exp(scores - jnp.max(scores, axis=1, keepdims=True))
        total = jnp.sum(weight, axis=1, keepdims=True)
        result = jnp.dot(weight.astype(BF16), v_ref[r], preferred_element_type=F32) / total
        for j in range(planes):
            mixed[j, every, :] = result[:, j * 128 : (j + 1) * 128]
    for i in range(heads * planes):
        h, j = divmod(i, planes)
        out_ref[:, i * 128 : (i + 1) * 128] = mixed[
            j, h * requests : (h + 1) * requests, :
        ].astype(BF16)
    for copy in copies:
        copy.wait()


def places(routes, levels, ks, span, capacity):
    rows = routes.shape[1]
    me = lax.axis_index("pool")
    slots = len(ks) * capacity
    slot = lax.broadcasted_iota(jnp.int32, (slots, 1), 0)
    expert = jnp.zeros((slots, 1), jnp.int32)
    for i, k in enumerate(ks):
        named = lax.bitwise_xor(me, k)
        if span > 1:
            named = lax.div(named, span)
        expert = jnp.where(slot >= i * capacity, named, expert)
    chosen = jnp.zeros((slots, rows), jnp.bool_)
    level = jnp.zeros((slots, rows), jnp.int32)
    for t in range(TOP):
        same = routes[t : t + 1, :] == expert
        chosen = jnp.logical_or(chosen, same)
        if levels is not None:
            level = level + jnp.where(same, levels[t : t + 1, :], 0)
    before = lax.broadcasted_iota(jnp.int32, (rows, rows), 0) < lax.broadcasted_iota(
        jnp.int32, (rows, rows), 1
    )
    rank = jnp.dot(
        jnp.where(chosen, 1.0, 0.0).astype(BF16),
        jnp.where(before, 1.0, 0.0).astype(BF16),
        preferred_element_type=F32,
    )
    place = lax.rem(slot, capacity).astype(F32)
    here = jnp.logical_and(chosen, rank == place)
    return here, level


def dispatch_kernel(pairs, span, capacity, routes_hbm, x_hbm, *refs):
    *outs, routes_ref, x_ref, sems = refs
    get_routes = pltpu.make_async_copy(routes_hbm, routes_ref, sems.at[0])
    get_x = pltpu.make_async_copy(x_hbm, x_ref, sems.at[1])
    get_routes.start()
    get_x.start()
    get_routes.wait()
    core = lax.axis_index("tp")
    half = x_ref.shape[1] // 2
    ks = [jnp.where(core == 0, a, b) for a, b in pairs] + [1, 0]
    here, _ = places(routes_ref[...], None, ks, span, capacity)
    picks = jnp.where(here, 1.0, 0.0).astype(BF16)
    m = len(pairs)
    get_x.wait()
    full = jnp.dot(picks, x_ref[...], preferred_element_type=F32)
    for i in range(m):
        outs[i][...] = full[i * capacity : (i + 1) * capacity].astype(BF16)
    outs[m + 1][...] = full[(m + 1) * capacity :].astype(BF16)
    mine = x_ref[:, pl.ds(pl.multiple_of(core * half, 128), half)]
    outs[m][...] = jnp.dot(
        picks[m * capacity : (m + 1) * capacity], mine, preferred_element_type=F32
    ).astype(BF16)


def expert_kernel(m, capacity, plan, *refs):
    blocks = refs[: 2 * m]
    share_mine, share_theirs, own = refs[2 * m : 2 * m + 3]
    held = sum(i >= 0 for ranges in plan for _, _, i in ranges)
    at = 2 * m + 3
    parts_held, refs = refs[at : at + held], refs[at + held :]
    gate_hbm, up_hbm, down_hbm, keep, give = refs[:5]
    x, rest_w, down_w, total, result, hidden, rest_sem, down_sem = refs[5:]
    core = lax.axis_index("tp")
    depth, width = x.shape[1], hidden.shape[1]
    half = depth // 2
    wide, ring = down_w.shape[1], down_w.shape[0]
    parts = width // wide

    fetches, place = {}, 0
    for ranges in zip(*plan):
        for j, (start, rows, i) in enumerate(ranges):
            source = (gate_hbm, up_hbm)[j]
            if i < 0:
                fetches[j, start] = (
                    place,
                    pltpu.make_async_copy(
                        source.at[pl.ds(start, rows)],
                        rest_w.at[pl.ds(place, rows)],
                        rest_sem.at[len(fetches)],
                    ),
                )
                place += rows

    def fetch(i):
        return pltpu.make_async_copy(
            down_hbm.at[pl.ds(i * wide, wide)], down_w.at[i % ring], down_sem.at[i]
        )

    queue = [copy for _, copy in fetches.values()] + [fetch(i) for i in range(min(ring, parts))]

    def ask(number):
        for copy in queue[:number]:
            copy.start()
        del queue[:number]

    ask(AHEAD)
    two = 2 * capacity
    for i in range(m):
        x[i * two : (i + 1) * two, :] = jnp.concatenate(
            [blocks[2 * i][...], blocks[2 * i + 1][...]], axis=0
        )
    for c, part in ((core, share_mine), (1 - core, share_theirs)):
        at = pl.ds(pl.multiple_of(c * half, 128), half)
        x[m * two : (m + 1) * two, at] = jnp.concatenate([part[...], own[:, at]], axis=0)
    for ranges in zip(*plan):
        for j, (start, rows, i) in enumerate(ranges):
            if i < 0:
                place, copy = fetches[j, start]
                copy.wait()
                ask(1)
                weight = rest_w[place : place + rows, :]
            else:
                weight = parts_held[i][...]
            term = jnp.dot(x[:, start : start + rows], weight, preferred_element_type=F32)
            total[j] = term if start == 0 else total[j] + term
    ask(len(queue))
    gate = total[0]
    hidden[...] = (gate / (1.0 + jnp.exp(-gate)) * total[1]).astype(BF16)
    for i in range(parts):
        fetch(i).wait()
        term = jnp.dot(
            hidden[:, i * wide : (i + 1) * wide], down_w[i % ring], preferred_element_type=F32
        )
        result[...] = term if i == 0 else result[...] + term
        if i + ring < parts:
            fetch(i + ring).start()
    n = m * capacity
    keep[:n, :] = result[:n, :]
    mine = pl.ds(pl.multiple_of(core * half, 128), half)
    theirs = pl.ds(pl.multiple_of((1 - core) * half, 128), half)
    keep[n:, :half] = result[2 * n : 2 * n + capacity, mine]
    keep[n:, half:] = result[2 * n + capacity :, mine]
    rest = jnp.concatenate(
        [result[2 * n : 2 * n + capacity, theirs], result[2 * n + capacity :, theirs]], axis=1
    )
    give[...] = jnp.concatenate([result[n : 2 * n, :], rest], axis=0).astype(BF16)


def sum_kernel(m, capacity, keep, got, *outs):
    both = keep[...] + got[...].astype(F32)
    half = keep.shape[1] // 2
    for i in range(m):
        outs[i][...] = both[i * capacity : (i + 1) * capacity].astype(BF16)
    outs[m][...] = both[m * capacity :, :half].astype(BF16)
    outs[m + 1][...] = both[m * capacity :, half:].astype(BF16)


def combine_kernel(pairs, span, capacity, routes_ref, level_ref, *refs):
    m = len(pairs)
    blocks, shared, own, out = refs[: 2 * m], refs[2 * m], refs[2 * m + 1], refs[2 * m + 2]
    core = lax.axis_index("tp")
    half = out.shape[1]
    ks = [jnp.where(core == 0, a, b) for a, b in pairs]
    ks += [jnp.where(core == 0, b, a) for a, b in pairs] + [1, 0]
    here, level = places(routes_ref[...], level_ref[...], ks, span, capacity)
    weight = jnp.where(here, level, 0).astype(F32) / 1024.0
    high = weight.astype(BF16)
    low = (weight - high.astype(F32)).astype(BF16)
    at = pl.ds(pl.multiple_of(core * half, 128), half)
    held = jnp.concatenate([b[:, at] for b in blocks] + [shared[...], own[...]], axis=0)
    dims = (((0,), (0,)), ((), ()))
    out[...] = (
        lax.dot_general(high, held, dims, preferred_element_type=F32)
        + lax.dot_general(low, held, dims, preferred_element_type=F32)
    ).astype(BF16)


def body(queries, keys, values, lengths, moe_input, routes, gate_level, w_gate, w_up, w_down):
    count = lax.axis_size("pool")
    span = count // EXPERTS
    rows_here, width = moe_input.shape
    capacity = rows_here // 2
    half = width // 2
    hid = w_gate.shape[2]
    pairs = distances(count)
    m = len(pairs)
    axes = ("pool", "tp")
    routes_t, level_t = routes.T, gate_level.T
    far = functools.partial(pltpu.with_memory_space_constraint, memory_space=pltpu.HBM)

    block = jax.ShapeDtypeStruct((capacity, width), BF16)
    half_block = jax.ShapeDtypeStruct((capacity, half), BF16)
    in_vmem = pl.BlockSpec(memory_space=VMEM)
    *sent, shared, own = pl.pallas_call(
        functools.partial(dispatch_kernel, pairs, span, capacity),
        out_shape=[block] * m + [half_block, block],
        in_specs=[pl.BlockSpec(memory_space=pltpu.HBM)] * 2,
        out_specs=[in_vmem] * (m + 2),
        scratch_shapes=[
            VMEM(routes_t.shape, jnp.int32),
            VMEM(moe_input.shape, BF16),
            pltpu.SemaphoreType.DMA((2,)),
        ],
        compiler_params=pltpu.CompilerParams(vmem_limit_bytes=(8 if m < 8 else 40) * MIB),
        name="dispatch",
    )(far(routes_t), far(moe_input))

    mine = [lax.ppermute(b, axes, route_of(count, pair)) for b, pair in zip(sent, pairs)]
    share_mine = lax.ppermute(shared, axes, route_of(count, (1, 1)))
    total_rows = count * capacity
    step = width // 14
    roomy = total_rows <= 64
    loads, plan = [], ([], [])
    for j, early in enumerate((width, HEAD) if roomy else (0, 0)):
        for start in range(0, width, step):
            index = -1
            if start < early:
                index = len(loads)
                loads.append((j, start, step))
            plan[j].append((start, step, index))
    gate_hbm, up_hbm, down_hbm = (far(w[0]) for w in (w_gate, w_up, w_down))
    requests, slots, size = keys.shape
    heads = queries.shape[1] // size
    in_hbm = pl.BlockSpec(memory_space=pltpu.HBM)
    early_bytes = 4 * requests * slots * size + 2 * hid * step * len(loads)
    context, *held = pl.pallas_call(
        functools.partial(attention_kernel, loads),
        out_shape=[jax.ShapeDtypeStruct(queries.shape, BF16)]
        + [VMEM((rows, hid), BF16) for _, _, rows in loads],
        in_specs=[in_hbm] * 6,
        out_specs=[in_vmem] * (1 + len(loads)),
        scratch_shapes=[
            pltpu.SMEM(lengths.shape, jnp.int32),
            VMEM(queries.shape, BF16),
            VMEM(keys.shape, BF16),
            VMEM(values.shape, BF16),
            VMEM((size // 128, heads * requests, 128), F32),
            VMEM((size // 128, heads * requests, 128), F32),
            pltpu.SemaphoreType.DMA((4,)),
            pltpu.SemaphoreType.DMA((max(1, len(loads)),)),
        ],
        compiler_params=pltpu.CompilerParams(vmem_limit_bytes=10 * MIB),
        cost_estimate=pl.CostEstimate(
            flops=4 * requests * heads * slots * size,
            bytes_accessed=early_bytes,
            transcendentals=requests * heads * slots,
        ),
        name="attention",
    )(far(lengths), far(queries), far(keys), far(values), gate_hbm, up_hbm)

    *mine, share_mine, context = lax.optimization_barrier((*mine, share_mine, context))
    theirs = [lax.ppermute(b, "tp", SWAP) for b in mine]
    share_theirs = lax.ppermute(share_mine, "tp", SWAP)

    fetched = 2 * 14 - len(loads)
    wide = 256 if hid % 256 == 0 else hid
    parts = hid // wide
    ring = min(parts, 3)
    weight_bytes = 2 * hid * (step * fetched + width)
    keep, give = pl.pallas_call(
        functools.partial(expert_kernel, m, capacity, plan),
        out_shape=[
            jax.ShapeDtypeStruct(((m + 1) * capacity, width), F32),
            jax.ShapeDtypeStruct(((m + 1) * capacity, width), BF16),
        ],
        in_specs=[in_vmem] * (2 * m + 3 + len(held)) + [in_hbm] * 3,
        out_specs=[in_vmem] * 2,
        scratch_shapes=[
            VMEM((total_rows, width), BF16),
            VMEM((step * fetched, hid), BF16),
            VMEM((ring, wide, width), BF16),
            VMEM((2, total_rows, hid), F32),
            VMEM((total_rows, width), F32),
            VMEM((total_rows, hid), BF16),
            pltpu.SemaphoreType.DMA((fetched,)),
            pltpu.SemaphoreType.DMA((parts,)),
        ],
        compiler_params=pltpu.CompilerParams(vmem_limit_bytes=(31 if roomy else 58) * MIB),
        cost_estimate=pl.CostEstimate(
            flops=2 * total_rows * 3 * width * hid, bytes_accessed=weight_bytes, transcendentals=0
        ),
        name="experts",
    )(*mine, *theirs, share_mine, share_theirs, own, *held, gate_hbm, up_hbm, down_hbm)

    got = lax.ppermute(give, "tp", SWAP)
    *back, share_back, own_back = pl.pallas_call(
        functools.partial(sum_kernel, m, capacity),
        out_shape=[block] * m + [half_block] * 2,
        in_specs=[in_vmem] * 2,
        out_specs=[in_vmem] * (m + 2),
        compiler_params=pltpu.CompilerParams(vmem_limit_bytes=(8 if m < 8 else 40) * MIB),
        name="sum",
    )(keep, got)

    mine = [lax.ppermute(b, axes, route_of(count, pair)) for b, pair in zip(back, pairs)]
    share_back = lax.ppermute(share_back, axes, route_of(count, (1, 1)))
    *mine, share_back = lax.optimization_barrier((*mine, share_back))
    theirs = [lax.ppermute(b, "tp", SWAP) for b in mine]
    moe_output = pl.pallas_call(
        functools.partial(combine_kernel, pairs, span, capacity),
        out_shape=jax.ShapeDtypeStruct((rows_here, half), BF16),
        in_specs=[in_vmem] * (2 * m + 4),
        out_specs=in_vmem,
        compiler_params=pltpu.CompilerParams(vmem_limit_bytes=(8 if m < 8 else 40) * MIB),
        name="combine",
    )(routes_t, level_t, *mine, *theirs, share_back, own_back)
    return (context, moe_output)


def solution(mesh):
    return jax.shard_map(
        body,
        mesh=mesh,
        in_specs=(
            P(("group", "pool"), "tp"),
            P(("group", "pool"), None, None),
            P(("group", "pool"), None, None),
            P(("group", "pool")),
            P(("group", "pool"), None),
            P(("group", "pool"), None),
            P(("group", "pool"), None),
            P("pool", None, "tp"),
            P("pool", None, "tp"),
            P("pool", "tp", None),
        ),
        out_specs=(P(("group", "pool"), "tp"), P(("group", "pool"), "tp")),
        check_vma=False,
    )
```

```python
import functools

import jax
import jax.numpy as jnp
from jax import lax
from jax.experimental import pallas as pl
from jax.experimental.pallas import tpu as pltpu
from jax.sharding import PartitionSpec as P

HDIM = 256
EXPERTS = 8
TOP = 3
MIB = 2**20
FIRST = 18
AHEAD = 4
SWAP = [(0, 1), (1, 0)]
VMEM = pltpu.VMEM
BF16 = jnp.bfloat16
F32 = jnp.float32


def distances(count):
    pairs, top = [], count // 2
    while top >= 2:
        half = top // 2
        pairs += [(top + i, top + half + i) for i in range(half)]
        top //= 2
    return pairs


def route_of(count, pair):
    return [
        (p * 2 + c, (p ^ pair[c]) * 2 + c) for p in range(count) for c in range(2)
    ]


def hold_kernel(loads, *refs):
    n = len(loads)
    weights, held, mark, sems = refs[:2], refs[-n - 2 : -2], refs[-2], refs[-1]
    copies = [
        pltpu.make_async_copy(weights[j].at[pl.ds(start, rows)], held[i], sems.at[i])
        for i, (j, start, rows) in enumerate(loads)
    ]
    for copy in copies:
        copy.start()
    mark[...] = jnp.zeros_like(mark)
    for copy in copies:
        copy.wait()


def attention_kernel(*refs):
    sources, out_ref = refs[:4], refs[4]
    lengths_ref, q_ref, k_ref, v_ref, packed, mixed, own_sems = refs[5:]
    own = [
        pltpu.make_async_copy(source, ref, own_sems.at[i])
        for i, (source, ref) in enumerate(zip(sources, (lengths_ref, q_ref, k_ref, v_ref)))
    ]
    for copy in own:
        copy.start()
    requests, slots, size = k_ref.shape
    heads = q_ref.shape[1] // size
    planes = packed.shape[0]
    own[0].wait()
    own[1].wait()
    for i in range(heads * planes):
        h, j = divmod(i, planes)
        packed[j, h * requests : (h + 1) * requests, :] = q_ref[:, i * 128 : (i + 1) * 128].astype(
            F32
        )
    own[2].wait()
    own[3].wait()
    for r in range(requests):
        every = pl.ds(r, heads, stride=requests)
        query = jnp.concatenate([packed[j, every, :] for j in range(planes)], axis=1).astype(BF16)
        scores = lax.dot_general(
            query, k_ref[r], (((1,), (1,)), ((), ())), preferred_element_type=F32
        ) * size ** (-0.5)
        live = lax.broadcasted_iota(jnp.int32, (1, slots), 1) < lengths_ref[r]
        scores = jnp.where(live, scores, -1e30)
        weight = jnp.exp(scores - jnp.max(scores, axis=1, keepdims=True))
        total = jnp.sum(weight, axis=1, keepdims=True)
        result = jnp.dot(weight.astype(BF16), v_ref[r], preferred_element_type=F32) / total
        for j in range(planes):
            mixed[j, every, :] = result[:, j * 128 : (j + 1) * 128]
    for i in range(heads * planes):
        h, j = divmod(i, planes)
        out_ref[:, i * 128 : (i + 1) * 128] = mixed[
            j, h * requests : (h + 1) * requests, :
        ].astype(BF16)


def places(routes, levels, ks, span, capacity):
    rows = routes.shape[1]
    me = lax.axis_index("pool")
    slots = len(ks) * capacity
    slot = lax.broadcasted_iota(jnp.int32, (slots, 1), 0)
    expert = jnp.zeros((slots, 1), jnp.int32)
    for i, k in enumerate(ks):
        named = lax.bitwise_xor(me, k)
        if span > 1:
            named = lax.div(named, span)
        expert = jnp.where(slot >= i * capacity, named, expert)
    chosen = jnp.zeros((slots, rows), jnp.bool_)
    level = jnp.zeros((slots, rows), jnp.int32)
    for t in range(TOP):
        same = routes[t : t + 1, :] == expert
        chosen = jnp.logical_or(chosen, same)
        if levels is not None:
            level = level + jnp.where(same, levels[t : t + 1, :], 0)
    before = lax.broadcasted_iota(jnp.int32, (rows, rows), 0) < lax.broadcasted_iota(
        jnp.int32, (rows, rows), 1
    )
    rank = jnp.dot(
        jnp.where(chosen, 1.0, 0.0).astype(BF16),
        jnp.where(before, 1.0, 0.0).astype(BF16),
        preferred_element_type=F32,
    )
    place = lax.rem(slot, capacity).astype(F32)
    here = jnp.logical_and(chosen, rank == place)
    return here, level


def dispatch_kernel(pairs, span, capacity, routes_hbm, x_hbm, *refs):
    *outs, routes_ref, x_ref, sems = refs
    get_routes = pltpu.make_async_copy(routes_hbm, routes_ref, sems.at[0])
    get_x = pltpu.make_async_copy(x_hbm, x_ref, sems.at[1])
    get_routes.start()
    get_x.start()
    get_routes.wait()
    core = lax.axis_index("tp")
    half = x_ref.shape[1] // 2
    ks = [jnp.where(core == 0, a, b) for a, b in pairs] + [1, 0]
    here, _ = places(routes_ref[...], None, ks, span, capacity)
    picks = jnp.where(here, 1.0, 0.0).astype(BF16)
    m = len(pairs)
    get_x.wait()
    full = jnp.dot(picks, x_ref[...], preferred_element_type=F32)
    for i in range(m):
        outs[i][...] = full[i * capacity : (i + 1) * capacity].astype(BF16)
    outs[m + 1][...] = full[(m + 1) * capacity :].astype(BF16)
    mine = x_ref[:, pl.ds(pl.multiple_of(core * half, 128), half)]
    outs[m][...] = jnp.dot(
        picks[m * capacity : (m + 1) * capacity], mine, preferred_element_type=F32
    ).astype(BF16)


def expert_kernel(m, capacity, plan, *refs):
    blocks = refs[: 2 * m]
    share_mine, share_theirs, own = refs[2 * m : 2 * m + 3]
    held = sum(i >= 0 for ranges in plan for _, _, i in ranges)
    at = 2 * m + 3
    parts_held, refs = refs[at : at + held], refs[at + held :]
    gate_hbm, up_hbm, down_hbm = refs[:3]
    keep, give, x, rest_w, down_w, total, result, hidden, rest_sem, down_sem = refs[-10:]
    core = lax.axis_index("tp")
    depth, width = x.shape[1], hidden.shape[1]
    half = depth // 2
    wide, ring = down_w.shape[1], down_w.shape[0]
    parts = width // wide

    fetches, slots = {}, rest_w.shape[0]
    for ranges in zip(*plan):
        for j, (start, rows, i) in enumerate(ranges):
            source = (gate_hbm, up_hbm)[j]
            if i < 0:
                place = len(fetches) % slots
                fetches[j, start] = (
                    place,
                    pltpu.make_async_copy(
                        source.at[pl.ds(start, rows)],
                        rest_w.at[place],
                        rest_sem.at[len(fetches)],
                    ),
                )

    def fetch(i):
        return pltpu.make_async_copy(
            down_hbm.at[pl.ds(i * wide, wide)], down_w.at[i % ring], down_sem.at[i]
        )

    queue = [copy for _, copy in fetches.values()] + [fetch(i) for i in range(min(ring, parts))]

    def ask(number):
        for copy in queue[:number]:
            copy.start()
        del queue[:number]

    ask(AHEAD)
    two = 2 * capacity
    for i in range(m):
        x[i * two : (i + 1) * two, :] = jnp.concatenate(
            [blocks[2 * i][...], blocks[2 * i + 1][...]], axis=0
        )
    for c, part in ((core, share_mine), (1 - core, share_theirs)):
        at = pl.ds(pl.multiple_of(c * half, 128), half)
        x[m * two : (m + 1) * two, at] = jnp.concatenate([part[...], own[:, at]], axis=0)
    for ranges in zip(*plan):
        for j, (start, rows, i) in enumerate(ranges):
            if i < 0:
                place, copy = fetches[j, start]
                copy.wait()
                ask(1)
                weight = rest_w[place]
            else:
                weight = parts_held[i][...]
            term = jnp.dot(x[:, start : start + rows], weight, preferred_element_type=F32)
            total[j] = term if start == 0 else total[j] + term
    ask(len(queue))
    gate = total[0]
    hidden[...] = (gate / (1.0 + jnp.exp(-gate)) * total[1]).astype(BF16)
    for i in range(parts):
        fetch(i).wait()
        term = jnp.dot(
            hidden[:, i * wide : (i + 1) * wide], down_w[i % ring], preferred_element_type=F32
        )
        result[...] = term if i == 0 else result[...] + term
        if i + ring < parts:
            fetch(i + ring).start()
    n = m * capacity
    keep[:n, :] = result[:n, :]
    mine = pl.ds(pl.multiple_of(core * half, 128), half)
    theirs = pl.ds(pl.multiple_of((1 - core) * half, 128), half)
    keep[n:, :half] = result[2 * n : 2 * n + capacity, mine]
    keep[n:, half:] = result[2 * n + capacity :, mine]
    rest = jnp.concatenate(
        [result[2 * n : 2 * n + capacity, theirs], result[2 * n + capacity :, theirs]], axis=1
    )
    give[...] = jnp.concatenate([result[n : 2 * n, :], rest], axis=0).astype(BF16)


def sum_kernel(m, capacity, keep, got, *outs):
    both = keep[...] + got[...].astype(F32)
    half = keep.shape[1] // 2
    for i in range(m):
        outs[i][...] = both[i * capacity : (i + 1) * capacity].astype(BF16)
    outs[m][...] = both[m * capacity :, :half].astype(BF16)
    outs[m + 1][...] = both[m * capacity :, half:].astype(BF16)


def combine_kernel(pairs, span, capacity, routes_ref, level_ref, *refs):
    m = len(pairs)
    blocks, shared, own, out = refs[: 2 * m], refs[2 * m], refs[2 * m + 1], refs[2 * m + 2]
    core = lax.axis_index("tp")
    half = out.shape[1]
    ks = [jnp.where(core == 0, a, b) for a, b in pairs]
    ks += [jnp.where(core == 0, b, a) for a, b in pairs] + [1, 0]
    here, level = places(routes_ref[...], level_ref[...], ks, span, capacity)
    weight = jnp.where(here, level, 0).astype(F32) / 1024.0
    high = weight.astype(BF16)
    low = (weight - high.astype(F32)).astype(BF16)
    at = pl.ds(pl.multiple_of(core * half, 128), half)
    held = jnp.concatenate([b[:, at] for b in blocks] + [shared[...], own[...]], axis=0)
    dims = (((0,), (0,)), ((), ()))
    out[...] = (
        lax.dot_general(high, held, dims, preferred_element_type=F32)
        + lax.dot_general(low, held, dims, preferred_element_type=F32)
    ).astype(BF16)


def body(queries, keys, values, lengths, moe_input, routes, gate_level, w_gate, w_up, w_down):
    count = lax.axis_size("pool")
    span = count // EXPERTS
    rows_here, width = moe_input.shape
    capacity = rows_here // 2
    half = width // 2
    hid = w_gate.shape[2]
    pairs = distances(count)
    m = len(pairs)
    axes = ("pool", "tp")
    routes_t, level_t = routes.T, gate_level.T
    far = functools.partial(pltpu.with_memory_space_constraint, memory_space=pltpu.HBM)

    block = jax.ShapeDtypeStruct((capacity, width), BF16)
    half_block = jax.ShapeDtypeStruct((capacity, half), BF16)
    in_vmem = pl.BlockSpec(memory_space=VMEM)
    *sent, shared, own = pl.pallas_call(
        functools.partial(dispatch_kernel, pairs, span, capacity),
        out_shape=[block] * m + [half_block, block],
        in_specs=[pl.BlockSpec(memory_space=pltpu.HBM)] * 2,
        out_specs=[in_vmem] * (m + 2),
        scratch_shapes=[
            VMEM(routes_t.shape, jnp.int32),
            VMEM(moe_input.shape, BF16),
            pltpu.SemaphoreType.DMA((2,)),
        ],
        compiler_params=pltpu.CompilerParams(vmem_limit_bytes=(8 if m < 8 else 40) * MIB),
        name="dispatch",
    )(far(routes_t), far(moe_input))

    mine = [lax.ppermute(b, axes, route_of(count, pair)) for b, pair in zip(sent, pairs)]
    share_mine = lax.ppermute(shared, axes, route_of(count, (1, 1)))
    total_rows = count * capacity
    step = width // 14
    roomy = total_rows <= 64
    order = [(j, start, step) for j in range(2) for start in range(0, width, step)]
    first = loads = order[:FIRST] if roomy else []
    plan = [
        [(start, step, loads.index((j, start, step)) if (j, start, step) in loads else -1)
         for start in range(0, width, step)]
        for j in range(2)
    ]
    gate_hbm, up_hbm, down_hbm = (far(w[0]) for w in (w_gate, w_up, w_down))
    in_hbm = pl.BlockSpec(memory_space=pltpu.HBM)

    def hold(blocks):
        *held, mark = pl.pallas_call(
            functools.partial(hold_kernel, blocks),
            out_shape=[VMEM((rows, hid), BF16) for _, _, rows in blocks]
            + [jax.ShapeDtypeStruct((8, 128), F32)],
            in_specs=[in_hbm] * 2,
            out_specs=[in_vmem] * (len(blocks) + 1),
            scratch_shapes=[pltpu.SemaphoreType.DMA((len(blocks),))],
            compiler_params=pltpu.CompilerParams(vmem_limit_bytes=MIB),
            cost_estimate=pl.CostEstimate(
                flops=0, bytes_accessed=2 * hid * step * len(blocks), transcendentals=0
            ),
            name="hold",
        )(gate_hbm, up_hbm)
        return held, mark

    held, marks = [], []
    if first:
        held, mark = hold(first)
        *mine, share_mine, mark = lax.optimization_barrier((*mine, share_mine, mark))
        marks = [mark]
    theirs = [lax.ppermute(b, "tp", SWAP) for b in mine]
    share_theirs = lax.ppermute(share_mine, "tp", SWAP)

    fetched = 2 * 14 - len(loads)
    wide = 256 if hid % 256 == 0 else hid
    parts = hid // wide
    ring = min(parts, 5)
    weight_bytes = 2 * hid * (step * fetched + width)
    keep, give = pl.pallas_call(
        functools.partial(expert_kernel, m, capacity, plan),
        out_shape=[
            jax.ShapeDtypeStruct(((m + 1) * capacity, width), F32),
            jax.ShapeDtypeStruct(((m + 1) * capacity, width), BF16),
        ],
        in_specs=[in_vmem] * (2 * m + 3 + len(held))
        + [in_hbm] * 3
        + [pl.BlockSpec(memory_space=pl.ANY)] * len(marks),
        out_specs=[in_vmem] * 2,
        scratch_shapes=[
            VMEM((total_rows, width), BF16),
            VMEM((min(fetched, AHEAD + 1), step, hid), BF16),
            VMEM((ring, wide, width), BF16),
            VMEM((2, total_rows, hid), F32),
            VMEM((total_rows, width), F32),
            VMEM((total_rows, hid), BF16),
            pltpu.SemaphoreType.DMA((fetched,)),
            pltpu.SemaphoreType.DMA((parts,)),
        ],
        compiler_params=pltpu.CompilerParams(vmem_limit_bytes=(28 if roomy else 58) * MIB),
        cost_estimate=pl.CostEstimate(
            flops=2 * total_rows * 3 * width * hid, bytes_accessed=weight_bytes, transcendentals=0
        ),
        name="experts",
    )(*mine, *theirs, share_mine, share_theirs, own, *held, gate_hbm, up_hbm, down_hbm, *marks)

    got = lax.ppermute(give, "tp", SWAP)
    *back, share_back, own_back = pl.pallas_call(
        functools.partial(sum_kernel, m, capacity),
        out_shape=[block] * m + [half_block] * 2,
        in_specs=[in_vmem] * 2,
        out_specs=[in_vmem] * (m + 2),
        compiler_params=pltpu.CompilerParams(vmem_limit_bytes=(8 if m < 8 else 40) * MIB),
        name="sum",
    )(keep, got)

    mine = [lax.ppermute(b, axes, route_of(count, pair)) for b, pair in zip(back, pairs)]
    share_back = lax.ppermute(share_back, axes, route_of(count, (1, 1)))

    requests, slots, size = keys.shape
    heads = queries.shape[1] // size
    lengths, own_back = lax.optimization_barrier((lengths, own_back))
    context = pl.pallas_call(
        attention_kernel,
        out_shape=jax.ShapeDtypeStruct(queries.shape, BF16),
        in_specs=[in_hbm] * 4,
        out_specs=in_vmem,
        scratch_shapes=[
            pltpu.SMEM(lengths.shape, jnp.int32),
            VMEM(queries.shape, BF16),
            VMEM(keys.shape, BF16),
            VMEM(values.shape, BF16),
            VMEM((size // 128, heads * requests, 128), F32),
            VMEM((size // 128, heads * requests, 128), F32),
            pltpu.SemaphoreType.DMA((4,)),
        ],
        compiler_params=pltpu.CompilerParams(vmem_limit_bytes=10 * MIB),
        cost_estimate=pl.CostEstimate(
            flops=4 * requests * heads * slots * size,
            bytes_accessed=4 * requests * slots * size,
            transcendentals=requests * heads * slots,
        ),
        name="attention",
    )(far(lengths), far(queries), far(keys), far(values))
    mine[0], share_back, context = lax.optimization_barrier((mine[0], share_back, context))
    theirs = [lax.ppermute(b, "tp", SWAP) for b in mine]
    moe_output = pl.pallas_call(
        functools.partial(combine_kernel, pairs, span, capacity),
        out_shape=jax.ShapeDtypeStruct((rows_here, half), BF16),
        in_specs=[in_vmem] * (2 * m + 4),
        out_specs=in_vmem,
        compiler_params=pltpu.CompilerParams(vmem_limit_bytes=(8 if m < 8 else 40) * MIB),
        name="combine",
    )(routes_t, level_t, *mine, *theirs, share_back, own_back)
    return (context, moe_output)


def solution(mesh):
    return jax.shard_map(
        body,
        mesh=mesh,
        in_specs=(
            P(("group", "pool"), "tp"),
            P(("group", "pool"), None, None),
            P(("group", "pool"), None, None),
            P(("group", "pool")),
            P(("group", "pool"), None),
            P(("group", "pool"), None),
            P(("group", "pool"), None),
            P("pool", None, "tp"),
            P("pool", None, "tp"),
            P("pool", "tp", None),
        ),
        out_specs=(P(("group", "pool"), "tp"), P(("group", "pool"), "tp")),
        check_vma=False,
    )
```

```python
import functools

import jax
import jax.numpy as jnp
from jax import lax
from jax.experimental import pallas as pl
from jax.experimental.pallas import tpu as pltpu
from jax.sharding import PartitionSpec as P

HDIM = 256
EXPERTS = 8
TOP = 3
MIB = 2**20
FIRST = 18
AHEAD = 4
SWAP = [(0, 1), (1, 0)]
VMEM = pltpu.VMEM
BF16 = jnp.bfloat16
F32 = jnp.float32


def distances(count):
    pairs, top = [], count // 2
    while top >= 2:
        half = top // 2
        pairs += [(top + i, top + half + i) for i in range(half)]
        top //= 2
    return pairs


def route_of(count, pair):
    return [
        (p * 2 + c, (p ^ pair[c]) * 2 + c) for p in range(count) for c in range(2)
    ]


def hold_kernel(loads, *refs):
    n = len(loads)
    weights, held, mark, sems = refs[:2], refs[-n - 2 : -2], refs[-2], refs[-1]
    copies = [
        pltpu.make_async_copy(weights[j].at[pl.ds(start, rows)], held[i], sems.at[i])
        for i, (j, start, rows) in enumerate(loads)
    ]
    for copy in copies:
        copy.start()
    mark[...] = jnp.zeros_like(mark)
    for copy in copies:
        copy.wait()


def attention_kernel(pairs, span, capacity, routes_ref, level_ref, *refs):
    sources, out_ref, gates_ref = refs[:4], refs[4], refs[5]
    lengths_ref, q_ref, k_ref, v_ref, packed, mixed, own_sems = refs[6:]
    own = [
        pltpu.make_async_copy(source, ref, own_sems.at[i])
        for i, (source, ref) in enumerate(zip(sources, (lengths_ref, q_ref, k_ref, v_ref)))
    ]
    for copy in own:
        copy.start()
    requests, slots, size = k_ref.shape
    heads = q_ref.shape[1] // size
    planes = packed.shape[0]
    own[0].wait()
    own[1].wait()
    for i in range(heads * planes):
        h, j = divmod(i, planes)
        packed[j, h * requests : (h + 1) * requests, :] = q_ref[:, i * 128 : (i + 1) * 128].astype(
            F32
        )
    own[2].wait()
    own[3].wait()
    for r in range(requests):
        every = pl.ds(r, heads, stride=requests)
        query = jnp.concatenate([packed[j, every, :] for j in range(planes)], axis=1).astype(BF16)
        scores = lax.dot_general(
            query, k_ref[r], (((1,), (1,)), ((), ())), preferred_element_type=F32
        ) * size ** (-0.5)
        live = lax.broadcasted_iota(jnp.int32, (1, slots), 1) < lengths_ref[r]
        scores = jnp.where(live, scores, -1e30)
        weight = jnp.exp(scores - jnp.max(scores, axis=1, keepdims=True))
        total = jnp.sum(weight, axis=1, keepdims=True)
        result = jnp.dot(weight.astype(BF16), v_ref[r], preferred_element_type=F32) / total
        for j in range(planes):
            mixed[j, every, :] = result[:, j * 128 : (j + 1) * 128]
    for i in range(heads * planes):
        h, j = divmod(i, planes)
        out_ref[:, i * 128 : (i + 1) * 128] = mixed[
            j, h * requests : (h + 1) * requests, :
        ].astype(BF16)
    core = lax.axis_index("tp")
    ks = [jnp.where(core == 0, a, b) for a, b in pairs]
    ks += [jnp.where(core == 0, b, a) for a, b in pairs] + [1, 0]
    here, level = places(routes_ref[...], level_ref[...], ks, span, capacity)
    weight = jnp.where(here, level, 0).astype(F32) / 1024.0
    high = weight.astype(BF16).astype(F32)
    gates_ref[...] = jnp.concatenate([high, weight - high], axis=1).T.astype(BF16)


def places(routes, levels, ks, span, capacity):
    rows = routes.shape[1]
    me = lax.axis_index("pool")
    slots = len(ks) * capacity
    slot = lax.broadcasted_iota(jnp.int32, (slots, 1), 0)
    expert = jnp.zeros((slots, 1), jnp.int32)
    for i, k in enumerate(ks):
        named = lax.bitwise_xor(me, k)
        if span > 1:
            named = lax.div(named, span)
        expert = jnp.where(slot >= i * capacity, named, expert)
    chosen = jnp.zeros((slots, rows), jnp.bool_)
    level = jnp.zeros((slots, rows), jnp.int32)
    for t in range(TOP):
        same = routes[t : t + 1, :] == expert
        chosen = jnp.logical_or(chosen, same)
        if levels is not None:
            level = level + jnp.where(same, levels[t : t + 1, :], 0)
    before = lax.broadcasted_iota(jnp.int32, (rows, rows), 0) < lax.broadcasted_iota(
        jnp.int32, (rows, rows), 1
    )
    rank = jnp.dot(
        jnp.where(chosen, 1.0, 0.0).astype(BF16),
        jnp.where(before, 1.0, 0.0).astype(BF16),
        preferred_element_type=F32,
    )
    place = lax.rem(slot, capacity).astype(F32)
    here = jnp.logical_and(chosen, rank == place)
    return here, level


def dispatch_kernel(pairs, span, capacity, routes_hbm, x_hbm, *refs):
    *outs, routes_ref, x_ref, sems = refs
    get_routes = pltpu.make_async_copy(routes_hbm, routes_ref, sems.at[0])
    get_x = pltpu.make_async_copy(x_hbm, x_ref, sems.at[1])
    get_routes.start()
    get_x.start()
    get_routes.wait()
    core = lax.axis_index("tp")
    half = x_ref.shape[1] // 2
    ks = [jnp.where(core == 0, a, b) for a, b in pairs] + [1, 0]
    here, _ = places(routes_ref[...], None, ks, span, capacity)
    picks = jnp.where(here, 1.0, 0.0).astype(BF16)
    m = len(pairs)
    get_x.wait()
    full = jnp.dot(picks, x_ref[...], preferred_element_type=F32)
    for i in range(m):
        outs[i][...] = full[i * capacity : (i + 1) * capacity].astype(BF16)
    outs[m + 1][...] = full[(m + 1) * capacity :].astype(BF16)
    mine = x_ref[:, pl.ds(pl.multiple_of(core * half, 128), half)]
    outs[m][...] = jnp.dot(
        picks[m * capacity : (m + 1) * capacity], mine, preferred_element_type=F32
    ).astype(BF16)


def expert_kernel(m, capacity, plan, *refs):
    blocks = refs[: 2 * m]
    share_mine, share_theirs, own = refs[2 * m : 2 * m + 3]
    held = sum(i >= 0 for ranges in plan for _, _, i in ranges)
    at = 2 * m + 3
    parts_held, refs = refs[at : at + held], refs[at + held :]
    gate_hbm, up_hbm, down_hbm = refs[:3]
    keep, give, x, rest_w, down_w, total, result, hidden, rest_sem, down_sem = refs[-10:]
    core = lax.axis_index("tp")
    depth, width = x.shape[1], hidden.shape[1]
    half = depth // 2
    wide, ring = down_w.shape[1], down_w.shape[0]
    parts = width // wide

    fetches, slots = {}, rest_w.shape[0]
    for ranges in zip(*plan):
        for j, (start, rows, i) in enumerate(ranges):
            source = (gate_hbm, up_hbm)[j]
            if i < 0:
                place = len(fetches) % slots
                fetches[j, start] = (
                    place,
                    pltpu.make_async_copy(
                        source.at[pl.ds(start, rows)],
                        rest_w.at[place],
                        rest_sem.at[len(fetches)],
                    ),
                )

    def fetch(i):
        return pltpu.make_async_copy(
            down_hbm.at[pl.ds(i * wide, wide)], down_w.at[i % ring], down_sem.at[i]
        )

    def fetch_last(c):
        at, rows = pl.ds(c * half, half), pl.ds((parts - 1) * wide, wide)
        return pltpu.make_async_copy(
            down_hbm.at[rows, at], down_w.at[(parts - 1) % ring, :, at], down_sem.at[parts - 1 + c]
        )

    def fetches_of(i):
        return [fetch(i)] if i < parts - 1 else [fetch_last(0), fetch_last(1)]

    queue = [copy for _, copy in fetches.values()]
    for i in range(min(ring, parts)):
        queue += fetches_of(i)

    def ask(number):
        for copy in queue[:number]:
            copy.start()
        del queue[:number]

    ask(AHEAD)
    two = 2 * capacity
    for i in range(m):
        x[i * two : (i + 1) * two, :] = jnp.concatenate(
            [blocks[2 * i][...], blocks[2 * i + 1][...]], axis=0
        )
    for c, part in ((core, share_mine), (1 - core, share_theirs)):
        at = pl.ds(pl.multiple_of(c * half, 128), half)
        x[m * two : (m + 1) * two, at] = jnp.concatenate([part[...], own[:, at]], axis=0)
    for ranges in zip(*plan):
        for j, (start, rows, i) in enumerate(ranges):
            if i < 0:
                place, copy = fetches[j, start]
                copy.wait()
                ask(1)
                weight = rest_w[place]
            else:
                weight = parts_held[i][...]
            term = jnp.dot(x[:, start : start + rows], weight, preferred_element_type=F32)
            total[j] = term if start == 0 else total[j] + term
    ask(len(queue))
    gate = total[0]
    hidden[...] = (gate / (1.0 + jnp.exp(-gate)) * total[1]).astype(BF16)
    for i in range(parts - 1):
        fetch(i).wait()
        term = jnp.dot(
            hidden[:, i * wide : (i + 1) * wide], down_w[i % ring], preferred_element_type=F32
        )
        result[...] = term if i == 0 else result[...] + term
        if i + ring < parts:
            for copy in fetches_of(i + ring):
                copy.start()
    for c in range(2):
        fetch_last(c).wait()
        at = slice(c * half, (c + 1) * half)
        term = jnp.dot(
            hidden[:, (parts - 1) * wide :],
            down_w[(parts - 1) % ring, :, at],
            preferred_element_type=F32,
        )
        result[:, at] = term if parts == 1 else result[:, at] + term
    n = m * capacity
    keep[:n, :] = result[:n, :]
    mine = pl.ds(pl.multiple_of(core * half, 128), half)
    theirs = pl.ds(pl.multiple_of((1 - core) * half, 128), half)
    keep[n:, :half] = result[2 * n : 2 * n + capacity, mine]
    keep[n:, half:] = result[2 * n + capacity :, mine]
    rest = jnp.concatenate(
        [result[2 * n : 2 * n + capacity, theirs], result[2 * n + capacity :, theirs]], axis=1
    )
    give[...] = jnp.concatenate([result[n : 2 * n, :], rest], axis=0).astype(BF16)


def sum_kernel(m, capacity, keep, got, *outs):
    both = keep[...] + got[...].astype(F32)
    half = keep.shape[1] // 2
    for i in range(m):
        outs[i][...] = both[i * capacity : (i + 1) * capacity].astype(BF16)
    outs[m][...] = both[m * capacity :, :half].astype(BF16)
    outs[m + 1][...] = both[m * capacity :, half:].astype(BF16)


def combine_kernel(gates_ref, *refs):
    *blocks, shared, own, out = refs
    core = lax.axis_index("tp")
    rows, half = out.shape
    at = pl.ds(pl.multiple_of(core * half, 128), half)
    held = jnp.concatenate([b[:, at] for b in blocks] + [shared[...], own[...]], axis=0)
    both = jnp.dot(gates_ref[...], held, preferred_element_type=F32)
    out[...] = (both[:rows] + both[rows:]).astype(BF16)


def body(queries, keys, values, lengths, moe_input, routes, gate_level, w_gate, w_up, w_down):
    count = lax.axis_size("pool")
    span = count // EXPERTS
    rows_here, width = moe_input.shape
    capacity = rows_here // 2
    half = width // 2
    hid = w_gate.shape[2]
    pairs = distances(count)
    m = len(pairs)
    axes = ("pool", "tp")
    routes_t, level_t = routes.T, gate_level.T
    far = functools.partial(pltpu.with_memory_space_constraint, memory_space=pltpu.HBM)

    block = jax.ShapeDtypeStruct((capacity, width), BF16)
    half_block = jax.ShapeDtypeStruct((capacity, half), BF16)
    in_vmem = pl.BlockSpec(memory_space=VMEM)
    *sent, shared, own = pl.pallas_call(
        functools.partial(dispatch_kernel, pairs, span, capacity),
        out_shape=[block] * m + [half_block, block],
        in_specs=[pl.BlockSpec(memory_space=pltpu.HBM)] * 2,
        out_specs=[in_vmem] * (m + 2),
        scratch_shapes=[
            VMEM(routes_t.shape, jnp.int32),
            VMEM(moe_input.shape, BF16),
            pltpu.SemaphoreType.DMA((2,)),
        ],
        compiler_params=pltpu.CompilerParams(vmem_limit_bytes=(8 if m < 8 else 40) * MIB),
        name="dispatch",
    )(far(routes_t), far(moe_input))

    mine = [lax.ppermute(b, axes, route_of(count, pair)) for b, pair in zip(sent, pairs)]
    share_mine = lax.ppermute(shared, axes, route_of(count, (1, 1)))
    total_rows = count * capacity
    step = width // 14
    roomy = total_rows <= 64
    order = [(j, start, step) for j in range(2) for start in range(0, width, step)]
    first = loads = order[:FIRST] if roomy else []
    plan = [
        [(start, step, loads.index((j, start, step)) if (j, start, step) in loads else -1)
         for start in range(0, width, step)]
        for j in range(2)
    ]
    gate_hbm, up_hbm, down_hbm = (far(w[0]) for w in (w_gate, w_up, w_down))
    in_hbm = pl.BlockSpec(memory_space=pltpu.HBM)

    def hold(blocks):
        *held, mark = pl.pallas_call(
            functools.partial(hold_kernel, blocks),
            out_shape=[VMEM((rows, hid), BF16) for _, _, rows in blocks]
            + [jax.ShapeDtypeStruct((8, 128), F32)],
            in_specs=[in_hbm] * 2,
            out_specs=[in_vmem] * (len(blocks) + 1),
            scratch_shapes=[pltpu.SemaphoreType.DMA((len(blocks),))],
            compiler_params=pltpu.CompilerParams(vmem_limit_bytes=MIB),
            cost_estimate=pl.CostEstimate(
                flops=0, bytes_accessed=2 * hid * step * len(blocks), transcendentals=0
            ),
            name="hold",
        )(gate_hbm, up_hbm)
        return held, mark

    held, marks = [], []
    if first:
        held, mark = hold(first)
        *mine, share_mine, mark = lax.optimization_barrier((*mine, share_mine, mark))
        marks = [mark]
    theirs = [lax.ppermute(b, "tp", SWAP) for b in mine]
    share_theirs = lax.ppermute(share_mine, "tp", SWAP)

    fetched = 2 * 14 - len(loads)
    wide = 256 if hid % 256 == 0 else hid
    parts = hid // wide
    ring = min(parts, 5)
    weight_bytes = 2 * hid * (step * fetched + width)
    keep, give = pl.pallas_call(
        functools.partial(expert_kernel, m, capacity, plan),
        out_shape=[
            jax.ShapeDtypeStruct(((m + 1) * capacity, width), F32),
            jax.ShapeDtypeStruct(((m + 1) * capacity, width), BF16),
        ],
        in_specs=[in_vmem] * (2 * m + 3 + len(held))
        + [in_hbm] * 3
        + [pl.BlockSpec(memory_space=pl.ANY)] * len(marks),
        out_specs=[in_vmem] * 2,
        scratch_shapes=[
            VMEM((total_rows, width), BF16),
            VMEM((min(fetched, AHEAD + 1), step, hid), BF16),
            VMEM((ring, wide, width), BF16),
            VMEM((2, total_rows, hid), F32),
            VMEM((total_rows, width), F32),
            VMEM((total_rows, hid), BF16),
            pltpu.SemaphoreType.DMA((fetched,)),
            pltpu.SemaphoreType.DMA((parts + 1,)),
        ],
        compiler_params=pltpu.CompilerParams(vmem_limit_bytes=(28 if roomy else 58) * MIB),
        cost_estimate=pl.CostEstimate(
            flops=2 * total_rows * 3 * width * hid, bytes_accessed=weight_bytes, transcendentals=0
        ),
        name="experts",
    )(*mine, *theirs, share_mine, share_theirs, own, *held, gate_hbm, up_hbm, down_hbm, *marks)

    got = lax.ppermute(give, "tp", SWAP)
    *back, share_back, own_back = pl.pallas_call(
        functools.partial(sum_kernel, m, capacity),
        out_shape=[block] * m + [half_block] * 2,
        in_specs=[in_vmem] * 2,
        out_specs=[in_vmem] * (m + 2),
        compiler_params=pltpu.CompilerParams(vmem_limit_bytes=(8 if m < 8 else 40) * MIB),
        name="sum",
    )(keep, got)

    mine = [lax.ppermute(b, axes, route_of(count, pair)) for b, pair in zip(back, pairs)]
    share_back = lax.ppermute(share_back, axes, route_of(count, (1, 1)))

    requests, slots, size = keys.shape
    heads = queries.shape[1] // size
    lengths, own_back = lax.optimization_barrier((lengths, own_back))
    context, gates = pl.pallas_call(
        functools.partial(attention_kernel, pairs, span, capacity),
        out_shape=[
            jax.ShapeDtypeStruct(queries.shape, BF16),
            jax.ShapeDtypeStruct((2 * rows_here, total_rows), BF16),
        ],
        in_specs=[in_vmem] * 2 + [in_hbm] * 4,
        out_specs=[in_vmem] * 2,
        scratch_shapes=[
            pltpu.SMEM(lengths.shape, jnp.int32),
            VMEM(queries.shape, BF16),
            VMEM(keys.shape, BF16),
            VMEM(values.shape, BF16),
            VMEM((size // 128, heads * requests, 128), F32),
            VMEM((size // 128, heads * requests, 128), F32),
            pltpu.SemaphoreType.DMA((4,)),
        ],
        compiler_params=pltpu.CompilerParams(vmem_limit_bytes=10 * MIB),
        cost_estimate=pl.CostEstimate(
            flops=4 * requests * heads * slots * size,
            bytes_accessed=4 * requests * slots * size,
            transcendentals=requests * heads * slots,
        ),
        name="attention",
    )(routes_t, level_t, far(lengths), far(queries), far(keys), far(values))
    mine[0], share_back, context = lax.optimization_barrier((mine[0], share_back, context))
    theirs = [lax.ppermute(b, "tp", SWAP) for b in mine]
    moe_output = pl.pallas_call(
        combine_kernel,
        out_shape=jax.ShapeDtypeStruct((rows_here, half), BF16),
        in_specs=[in_vmem] * (2 * m + 3),
        out_specs=in_vmem,
        compiler_params=pltpu.CompilerParams(vmem_limit_bytes=(8 if m < 8 else 40) * MIB),
        name="combine",
    )(gates, *mine, *theirs, share_back, own_back)
    return (context, moe_output)


def solution(mesh):
    return jax.shard_map(
        body,
        mesh=mesh,
        in_specs=(
            P(("group", "pool"), "tp"),
            P(("group", "pool"), None, None),
            P(("group", "pool"), None, None),
            P(("group", "pool")),
            P(("group", "pool"), None),
            P(("group", "pool"), None),
            P(("group", "pool"), None),
            P("pool", None, "tp"),
            P("pool", None, "tp"),
            P("pool", "tp", None),
        ),
        out_specs=(P(("group", "pool"), "tp"), P(("group", "pool"), "tp")),
        check_vma=False,
    )
```
